512 devices in a mesh: section: 8 (over y), tensor: 32 (over x_hi, z, core), dp: 2 (over x_lo).
Axes of the slice: x: 4 (x_hi: 2, x_lo: 2; x = x_hi * 2 + x_lo), y: 8, z: 8, core: 2. Of those that a mesh axis runs over, the one named last changes fastest.
Arguments:
- acts: bfloat16 [8, 2, 256, 3328], P('section', None, ('tensor', 'dp')), may hold values from -6 to 6
- cotangent: bfloat16 [8, 2, 256, 3328], P('section', None, ('tensor', 'dp')), may hold values from -6 to 6
- w_in: bfloat16 [8, 3328, 8960], P('section', 'dp', 'tensor'), may hold values from -0.109375 to 0.109375
- w_out: bfloat16 [8, 8960, 3328], P('section', 'tensor', 'dp'), may hold values from -0.0625 to 0.0625
Outputs:
- result: bfloat16 [8, 2, 256, 3328], P('section', None, ('tensor', 'dp'))
- d_acts: bfloat16 [8, 2, 256, 3328], P('section', None, ('tensor', 'dp'))
- grad_in: bfloat16 [8, 3328, 8960], P('section', 'dp', 'tensor')
- grad_out: bfloat16 [8, 8960, 3328], P('section', 'tensor', 'dp')
The draws below stay inside these ranges and needn't reach their ends.
All inputs are finite; a program needn't handle non-finite values.
Results may differ from the reference program's by a relative error of at most 0.015.
Values may be sent and summed in bfloat16 or wider, within the bound.
A program may use at most 64 MiB of HBM per device.

```python
import jax
import jax.numpy as jnp
from jax import lax

D = 3328
FF = 8960
ROWS = 128
SECTIONS = 8
HID_DEV = 280
N_DP = 2


def steps_of(key, extent, cuts, smallest, top_value):
    loudness = 1.0
    for axis_at, parts in cuts:
        draws = jax.random.uniform(jax.random.fold_in(jax.random.fold_in(key, 6), axis_at), (parts,), jnp.float32, smallest / len(cuts), top_value / len(cuts))
        loudness = loudness * jnp.repeat(jnp.exp(draws), extent[axis_at] // parts).reshape((-1,) + (1,) * (len(extent) - 1 - axis_at))
    return loudness


def scatter_about(rng, extent, scale, most, shards=(), held_as=jnp.bfloat16):
    values = jax.random.normal(rng, extent, jnp.float32) * scale
    if len(shards) > 0:
        values = steps_of(rng, extent, shards, -0.22, 0.18) * values
    return jnp.clip(values, min=-most, max=most).astype(held_as)


def setup_inputs(seed: int = 0) -> dict:
    seeds = jax.random.split(jax.random.key(seed), 5)
    acts = scatter_about(seeds[0], (SECTIONS, 2, N_DP * ROWS, D), 1.0, 6.0, ((0, 8), (2, 64)))
    cotangent = scatter_about(seeds[1], (SECTIONS, 2, N_DP * ROWS, D), 1.0, 6.0, ((0, 8), (2, 64)))
    w_in = scatter_about(seeds[2], (SECTIONS, D, FF), D ** -0.5, 0.109375, ((0, 8), (1, 2), (2, 32)))
    w_out = scatter_about(seeds[3], (SECTIONS, FF, D), FF ** -0.5, 0.0625, ((0, 8), (1, 32), (2, 2)))
    return {"acts": acts, "cotangent": cotangent, "w_in": w_in, "w_out": w_out}


def block_sum(left, right_blocks):
    count_rows = left.shape[0]
    width = right_blocks.shape[2]

    def add_block(total, pair):
        piece, weight = pair
        term = jnp.dot(piece, weight, preferred_element_type=jnp.float32)
        term = lax.optimization_barrier(term.astype(jnp.bfloat16))
        return (total + term.astype(jnp.float32), None)
    total, _ = lax.scan(add_block, jnp.zeros((count_rows, width), jnp.float32), (jnp.swapaxes(left, 0, 1), right_blocks))
    return total

def layer(rows, grads, weight_in, weight_out):
    count_rows = rows.shape[0]
    blocks = weight_in.shape[1] // HID_DEV
    hidden = jnp.dot(rows, weight_in, preferred_element_type=jnp.float32)
    act, gelu_back = jax.vjp(jax.nn.gelu, hidden)
    act_b = act.astype(jnp.bfloat16)
    branch = block_sum(act_b.reshape(count_rows, blocks, HID_DEV), weight_out.reshape(blocks, HID_DEV, D))
    outputs = (rows.astype(jnp.float32) + branch).astype(jnp.bfloat16)
    d_act = jnp.dot(grads, weight_out.T, preferred_element_type=jnp.float32)
    d_hid = gelu_back(d_act)[0].astype(jnp.bfloat16)
    back = block_sum(d_hid.reshape(count_rows, blocks, HID_DEV), weight_in.T.reshape(blocks, HID_DEV, D))
    d_rows = (grads.astype(jnp.float32) + back).astype(jnp.bfloat16)
    g_in = jnp.dot(rows.T, d_hid, preferred_element_type=jnp.float32).astype(jnp.bfloat16)
    g_out = jnp.dot(act_b.T, grads, preferred_element_type=jnp.float32).astype(jnp.bfloat16)
    return (outputs, d_rows, g_in, g_out)

def reference(acts, cotangent, w_in, w_out):
    sections = acts.shape[0]
    half = acts.shape[2]

    def one_section(index):
        mirror = sections - 1 - index
        rows = jnp.concatenate([acts[index, 0], acts[mirror, 1]], 0)
        grads = jnp.concatenate([cotangent[index, 0], cotangent[mirror, 1]], 0)
        outputs, d_rows, g_in, g_out = layer(rows, grads, w_in[index], w_out[index])
        return (outputs[:half], outputs[half:], d_rows[:half], d_rows[half:], g_in, g_out)
    res = lax.map(one_section, jnp.arange(sections, dtype=jnp.int32))
    result = jnp.stack([res[0], res[1][::-1]], 1)
    d_acts = jnp.stack([res[2], res[3][::-1]], 1)
    return (result, d_acts, res[4], res[5])
```

```python
import jax
import jax.numpy as jnp
from jax import lax
from jax.experimental import pallas as pl
from jax.experimental.pallas import tpu as pltpu
from jax.sharding import PartitionSpec as P

MESH = pl.DeviceIdType.MESH
BF, F32 = jnp.bfloat16, jnp.float32
RING = 8
HOPS = RING // 2
BLOCK = 32
GROUP = 4 * BLOCK
HALF = 2 * BLOCK
COPIES = 80
ROOT = 0.7978845608028654
CUBE = 0.044715


def nt(a, b):
    return lax.dot_general(a, b, (((1,), (1,)), ((), ())), preferred_element_type=F32)


def nn(a, b):
    return lax.dot_general(a, b, (((1,), (0,)), ((), ())), preferred_element_type=F32)


def tn(a, b):
    return lax.dot_general(a, b, (((0,), (0,)), ((), ())), preferred_element_type=F32)


def kernel(
    x_in, c_in, w1_hbm, w2_hbm,
    res, dx, gi_hbm, go_hbm,
    xs, xr, cs, cr, ys, yr, ds, dr, wide, X, C, w1, w2, gi, go,
    h_own, h_out, h_in, e_own, e_out, e_in, slope, act, grd,
    po, ps, pr, sp, rp, px, pxr, qo, qs, qr, sq, rq, qx, qxr,
    send_sem, recv_sem, local_sem,
):
    s, t, p = (lax.axis_index(a) for a in ("section", "tensor", "dp"))
    sections = lax.axis_size("section")
    core = t % 2
    z = (t // 2) % RING
    x_hi = t // (2 * RING)
    turn = 1 - 2 * core

    def at_z(step):
        return (s, x_hi * 2 * RING + ((z + RING + step) % RING) * 2 + core, p)

    up, down = at_z(turn), at_z(-turn)
    sib = (s, t + turn, p)
    across = (s, (t + 2 * RING) % (4 * RING), p)
    pair = (s, t, 1 - p)
    far = (sections - 1 - s, t, p)
    far_pair = (sections - 1 - s, t, 1 - p)
    half = w1.shape[1]

    barrier = pltpu.get_barrier_semaphore()
    peers = (up, down, sib, across, pair, far, far_pair)
    for peer in peers:
        pl.semaphore_signal(barrier, inc=1, device_id=peer, device_id_type=MESH)

    load1 = pltpu.make_async_copy(w1_hbm, w1, local_sem.at[0])
    load2 = pltpu.make_async_copy(w2_hbm, w2, local_sem.at[1])
    load1.start()
    load2.start()

    sent = []
    count = [0]

    def ticket():
        count[0] += 1
        return count[0] - 1

    def send(src, dst, device, n):
        copy = pltpu.make_async_remote_copy(
            src_ref=src, dst_ref=dst, send_sem=send_sem.at[n], recv_sem=recv_sem.at[n],
            device_id=device, device_id_type=MESH,
        )
        copy.start()
        sent.append(copy)

    def arrived(dst, device, n):
        pltpu.make_async_remote_copy(
            src_ref=dst, dst_ref=dst, send_sem=send_sem.at[n], recv_sem=recv_sem.at[n],
            device_id=device, device_id_type=MESH,
        ).wait_recv()

    for source, stage in ((x_in, xs), (c_in, cs)):
        for d in range(2):
            for h in range(2):
                stage[d, h] = source[d, :, h * half : (h + 1) * half]
    pl.semaphore_wait(barrier, len(peers))

    routes = ((0, 1, pair), (1, 0, far), (1, 1, far_pair))

    def spread(stage, land):
        numbers = [ticket() for _ in routes]
        for n, (d, rel, device) in zip(numbers, routes):
            other = p + rel - 2 * rel * p
            send(stage.at[d, other], land.at[d, p], device, n)
        land[0, p] = stage[0, p]
        return numbers

    def landed(land, numbers):
        for n, (d, rel, device) in zip(numbers, routes):
            arrived(land.at[d, p + rel - 2 * rel * p], device, n)

    x_spread = spread(xs, xr)
    c_spread = spread(cs, cr)

    ZERO = 13 * BLOCK

    def rows(ref, at, n):
        return ref.at[pl.ds(at, n)]

    def own_rows(land, numbers, buf):
        landed(land, numbers)
        for d in range(2):
            for q in range(2):
                at = (d * 2 + q) * 4
                wide[at : at + 4, :] = land[d, q].astype(F32)
        buf[ZERO : ZERO + 16, :] = wide[...].astype(BF)
        n = ticket()
        send(rows(buf, ZERO, 16), rows(buf, ZERO + 16, 16), across, n)
        return n

    class Gather:
        def __init__(self, buf):
            self.buf = buf
            self.a = [ticket() for _ in range(HOPS)]
            self.b = [ticket() for _ in range(HOPS - 1)]
            self.s = [ticket() for _ in range(HOPS + 1)]

        def place(self, k, which):
            if k == 0:
                return rows(self.buf, ZERO, BLOCK)
            return rows(self.buf, GROUP * (k - 1) + BLOCK * which, BLOCK)

        def start(self, n):
            arrived(rows(self.buf, ZERO + 16, 16), across, n)
            self.forward(0)
            send(self.place(0, 0), rows(self.buf, ZERO + HALF, BLOCK), sib, self.s[HOPS])

        def forward(self, k):
            if k < HOPS:
                send(self.place(k, 0), self.place(k + 1, 0), up, self.a[k])
            if k < HOPS - 1:
                send(self.place(k, 1), self.place(k + 1, 1), down, self.b[k])

        def step(self, k):
            arrived(self.place(k, 0), up, self.a[k - 1])
            if k < HOPS:
                arrived(self.place(k, 1), down, self.b[k - 1])
            self.forward(k)
            at, n = GROUP * (k - 1), HALF if k < HOPS else BLOCK
            send(rows(self.buf, at, n), rows(self.buf, at + HALF, n), sib, self.s[k - 1])

        def group(self, k):
            at, n = GROUP * (k - 1) + HALF, HALF if k < HOPS else BLOCK
            arrived(rows(self.buf, at, n), sib, self.s[k - 1])
            if k == HOPS:
                arrived(rows(self.buf, ZERO + HALF, BLOCK), sib, self.s[HOPS])

    class Inner:
        def __init__(self, gather, weight, own, out, inn):
            self.gather, self.weight = gather, weight
            self.own, self.out, self.inn = own, out, inn
            self.n = [ticket() for _ in range(HOPS)]

        def make(self, k):
            self.gather.group(k)
            at = GROUP * (k - 1)
            part = nt(self.gather.buf[at : at + GROUP, :], self.weight[...])
            self.own[at : at + GROUP, :] = part
            self.out[at : at + GROUP, :] = part.astype(BF)
            send(rows(self.out, at, GROUP), rows(self.inn, at, GROUP), pair, self.n[k - 1])

        def total(self, k):
            at = GROUP * (k - 1)
            arrived(rows(self.inn, at, GROUP), pair, self.n[k - 1])
            return self.own[at : at + GROUP, :] + self.inn[at : at + GROUP, :].astype(F32)

    class Scatter:
        def __init__(self, left, weight, own, out, inn, go_on, come, edge, edge_in, base, stage, land, dest):
            self.left, self.weight = left, weight
            self.own, self.out, self.inn = own, out, inn
            self.go_on, self.come = go_on, come
            self.edge, self.edge_in, self.base = edge, edge_in, base
            self.stage, self.land, self.dest = stage, land, dest
            self.s = [ticket() for _ in range(HOPS)]
            self.a = [ticket() for _ in range(HOPS)]
            self.b = [ticket() for _ in range(HOPS - 1)]
            self.x = ticket()

        def make(self, k):
            at = GROUP * (k - 1)
            term = nn(self.left[at : at + GROUP, :], self.weight[...])
            to = HALF * (k - 1)
            self.out[to : to + HALF, :] = term[HALF:, :].astype(BF)
            send(rows(self.out, to, HALF), rows(self.inn, to, HALF), sib, self.s[k - 1])
            self.own[to : to + HALF, :] = term[:HALF, :]

        def sums(self, at, n):
            return self.own[at : at + n, :] + self.inn[at : at + n, :].astype(F32)

        def step(self, k):
            to = HALF * (k - 1)
            arrived(rows(self.inn, to, HALF), sib, self.s[k - 1])
            if k < HOPS:
                arrived(rows(self.come, to + HALF, BLOCK), down, self.a[k])
            first = self.sums(to, BLOCK)
            if k < HOPS:
                first += self.come[to + HALF : to + HALF + BLOCK, :].astype(F32)
            self.go_on[to : to + BLOCK, :] = first.astype(BF)
            send(rows(self.go_on, to, BLOCK), rows(self.come, to, BLOCK), down, self.a[k - 1])
            if k < HOPS:
                mid = to + BLOCK
                second = self.sums(mid, BLOCK)
                if k < HOPS - 1:
                    arrived(rows(self.come, mid + HALF, BLOCK), up, self.b[k])
                    second += self.come[mid + HALF : mid + HALF + BLOCK, :].astype(F32)
                self.go_on[mid : mid + BLOCK, :] = second.astype(BF)
                send(rows(self.go_on, mid, BLOCK), rows(self.come, mid, BLOCK), up, self.b[k - 1])

        def edges(self):
            arrived(rows(self.come, 0, BLOCK), down, self.a[0])
            arrived(rows(self.come, BLOCK, BLOCK), up, self.b[0])
            at = HALF * HOPS - BLOCK
            all_here = self.sums(at, BLOCK) + self.come[0:BLOCK, :].astype(F32)
            all_here += self.come[BLOCK:HALF, :].astype(F32)
            self.edge[...] = all_here[16:, :].astype(BF)
            send(self.edge, self.edge_in, across, self.x)
            self.own[at : at + 16, :] = all_here[:16, :]

        def finish(self):
            arrived(self.edge_in, across, self.x)
            at = HALF * HOPS - BLOCK
            wide[...] = (
                self.own[at : at + 16, :]
                + self.edge_in[...].astype(F32)
                + self.base[ZERO : ZERO + 16, :].astype(F32)
            )
            for d in range(2):
                for q in range(2):
                    start = (d * 2 + q) * 4
                    self.stage[d, q] = wide[start : start + 4, :].astype(BF)
            self.numbers = spread(self.stage, self.land)

        def deliver(self):
            landed(self.land, self.numbers)
            for d in range(2):
                for h in range(2):
                    self.dest[d, :, h * half : (h + 1) * half] = self.land[d, h]

    def bend(k):
        at = GROUP * (k - 1)
        v = hid.total(k)
        square = v * v
        th = jnp.tanh(ROOT * (v + CUBE * (square * v)))
        gate = 0.5 * (1.0 + th)
        act[at : at + GROUP, :] = (v * gate).astype(BF)
        slope[at : at + GROUP, :] = gate + 0.5 * v * (1.0 - th * th) * (
            ROOT * (1.0 + 3.0 * CUBE * square)
        )

    def back(k):
        at = GROUP * (k - 1)
        grd[at : at + GROUP, :] = (err.total(k) * slope[at : at + GROUP, :]).astype(BF)

    gx, gc = Gather(X), Gather(C)
    hid = Inner(gx, w1, h_own, h_out, h_in)
    err = Inner(gc, w2, e_own, e_out, e_in)

    nx = own_rows(xr, x_spread, X)
    nc = own_rows(cr, c_spread, C)
    gx.start(nx)
    load1.wait()
    load2.wait()
    gx.step(1)
    gc.start(nc)
    gx.step(2)
    gc.step(1)
    hid.make(1)
    gx.step(3)
    gc.step(2)
    hid.make(2)
    gx.step(4)
    gc.step(3)
    hid.make(3)
    hid.make(4)
    err.make(1)
    err.make(2)
    bend(1)
    bend(2)
    bend(3)
    gc.step(4)
    err.make(3)

    sc_p = Scatter(act, w2, po, ps, pr, sp, rp, px, pxr, X, ys, yr, res)
    sc_q = Scatter(grd, w1, qo, qs, qr, sq, rq, qx, qxr, C, ds, dr, dx)

    bend(4)
    sc_p.make(4)
    sc_p.make(3)
    err.make(4)
    sc_p.step(4)
    sc_p.make(2)
    sc_p.make(1)
    back(1)
    back(2)
    back(3)
    sc_p.step(3)
    back(4)
    sc_q.make(4)
    sc_q.make(3)
    sc_q.step(4)
    sc_p.step(2)
    sc_q.make(2)
    sc_q.make(1)
    sc_q.step(3)
    go[...] = tn(act[...], C[...]).astype(BF)
    store1 = pltpu.make_async_copy(go, go_hbm, local_sem.at[2])
    store1.start()
    sc_p.step(1)
    sc_q.step(2)
    gi[...] = tn(grd[...], X[...]).astype(BF)
    store2 = pltpu.make_async_copy(gi, gi_hbm, local_sem.at[3])
    store2.start()
    sc_p.edges()
    sc_q.step(1)
    sc_p.finish()
    sc_q.edges()
    sc_q.finish()
    sc_p.deliver()
    sc_q.deliver()
    for copy in sent:
        copy.wait_send()
    store1.wait()
    store2.wait()


def on_device(acts, cotangent, w_in, w_out):
    _, hidden, half = w_out.shape
    d_model = 2 * half
    every = HOPS * GROUP
    v = pltpu.VMEM
    stage = v((2, 2, 4, half), BF)
    inner = [v((every, hidden), F32), v((every, hidden), BF), v((every, hidden), BF)]
    own = HALF * HOPS
    outer = [v((own, half), F32)] + [v((own, half), BF)] * 4 + [v((16, half), BF)] * 2
    any_place = pl.BlockSpec(memory_space=pl.ANY)
    here = pl.BlockSpec(memory_space=pltpu.VMEM)
    result, d_acts, g_in, g_out = pl.pallas_call(
        kernel,
        out_shape=(
            jax.ShapeDtypeStruct((2, 4, d_model), BF),
            jax.ShapeDtypeStruct((2, 4, d_model), BF),
            jax.ShapeDtypeStruct((hidden, half), BF),
            jax.ShapeDtypeStruct((hidden, half), BF),
        ),
        in_specs=[here, here, any_place, any_place],
        out_specs=(here, here, any_place, any_place),
        scratch_shapes=[stage] * 8
        + [v((16, half), F32)]
        + [v((every, half), BF)] * 2
        + [v((hidden, half), BF)] * 4
        + inner * 2
        + [v((every, hidden), F32), v((every, hidden), BF), v((every, hidden), BF)]
        + outer * 2
        + [
            pltpu.SemaphoreType.DMA((COPIES,)),
            pltpu.SemaphoreType.DMA((COPIES,)),
            pltpu.SemaphoreType.DMA((4,)),
        ],
        compiler_params=pltpu.CompilerParams(
            collective_id=0, has_side_effects=True, vmem_limit_bytes=48 * 1024 * 1024
        ),
        cost_estimate=pl.CostEstimate(
            flops=12 * every * hidden * half, bytes_accessed=8 * hidden * half, transcendentals=every * hidden
        ),
    )(acts[0], cotangent[0], jnp.swapaxes(w_in[0], 0, 1), w_out[0])
    return (result[None], d_acts[None], jnp.swapaxes(g_in, 0, 1)[None], g_out[None])


def solution(mesh):
    placed = (
        P("section", None, ("tensor", "dp"), None),
        P("section", None, ("tensor", "dp"), None),
        P("section", "dp", "tensor"),
        P("section", "tensor", "dp"),
    )
    return jax.shard_map(on_device, mesh=mesh, in_specs=placed, out_specs=placed, check_vma=False)
```

```python
import jax
import jax.numpy as jnp
from jax import lax
from jax.experimental import pallas as pl
from jax.experimental.pallas import tpu as pltpu
from jax.sharding import PartitionSpec as P

MESH = pl.DeviceIdType.MESH
BF, F32 = jnp.bfloat16, jnp.float32
RING = 8
HOPS = RING // 2
BLOCK = 32
PART = BLOCK // 2
EVERY = 2 * RING * BLOCK
COPIES = 114
ROOT = 0.7978845608028654
CUBE = 0.044715


def group_own(k):
    return BLOCK if k in (0, HOPS) else 2 * BLOCK


def own_at(k):
    return sum(group_own(i) for i in range(k))


def group_at(k):
    return 2 * own_at(k)


def nt(a, b):
    return lax.dot_general(a, b, (((1,), (1,)), ((), ())), preferred_element_type=F32)


def nn(a, b):
    return lax.dot_general(a, b, (((1,), (0,)), ((), ())), preferred_element_type=F32)


def tn(a, b):
    return lax.dot_general(a, b, (((0,), (0,)), ((), ())), preferred_element_type=F32)


def kernel(
    x_hbm, c_hbm, w1_hbm, w2_hbm,
    res, dx, gi_hbm, go_hbm,
    x_in, c_in, xs, xr, cs, cr, ys, yr, ds, dr, wide, X, C, w1, w2, gi, go,
    h_own, h_out, h_in, e_own, e_out, e_in, slope, act, grd,
    po, ps, pr, sp, rp, qo, qs, qr, sq, rq,
    send_sem, recv_sem, local_sem,
):
    s, t, p = (lax.axis_index(a) for a in ("section", "tensor", "dp"))
    sections = lax.axis_size("section")
    core = t % 2
    z = (t // 2) % RING
    x_hi = t // (2 * RING)
    turn = 1 - 2 * core

    def at_z(step):
        return (s, x_hi * 2 * RING + ((z + RING + step) % RING) * 2 + core, p)

    up, down, up2, down2 = at_z(turn), at_z(-turn), at_z(2 * turn), at_z(-2 * turn)
    sib = (s, t + turn, p)
    other_t = (t + 2 * RING) % (4 * RING)
    mirror = sections - 1 - s
    routes = [
        (d, x, rel, ((s, mirror)[d], (t, other_t)[x], p + rel - 2 * rel * p))
        for d in range(2)
        for x in range(2)
        for rel in range(2)
        if d + x + rel > 0
    ]
    pair = routes[0][3]
    half = w1.shape[1]

    barrier = pltpu.get_barrier_semaphore()
    peers = [up, down, up2, down2, sib] + [route[3] for route in routes]
    for peer in peers:
        pl.semaphore_signal(barrier, inc=1, device_id=peer, device_id_type=MESH)

    load_x = pltpu.make_async_copy(x_hbm, x_in, local_sem.at[4])
    load_c = pltpu.make_async_copy(c_hbm, c_in, local_sem.at[5])
    load_x.start()
    load_c.start()
    load1 = pltpu.make_async_copy(w1_hbm, w1, local_sem.at[0])
    load2 = pltpu.make_async_copy(w2_hbm, w2, local_sem.at[1])
    load1.start()
    load2.start()

    sent = []
    count = [0]

    def ticket():
        count[0] += 1
        return count[0] - 1

    def send(src, dst, device, n):
        copy = pltpu.make_async_remote_copy(
            src_ref=src, dst_ref=dst, send_sem=send_sem.at[n], recv_sem=recv_sem.at[n],
            device_id=device, device_id_type=MESH,
        )
        copy.start()
        sent.append(copy)

    def arrived(dst, device, n):
        pltpu.make_async_remote_copy(
            src_ref=dst, dst_ref=dst, send_sem=send_sem.at[n], recv_sem=recv_sem.at[n],
            device_id=device, device_id_type=MESH,
        ).wait_recv()

    for load, source, stage in ((load_x, x_in, xs), (load_c, c_in, cs)):
        load.wait()
        for d in range(2):
            for h in range(2):
                stage[d, h] = source[d, :, h * half : (h + 1) * half]
    pl.semaphore_wait(barrier, len(peers))

    def spread(land, part, piece):
        numbers = {}
        for d, x, rel, device in routes:
            if d == part:
                numbers[(x, rel)] = ticket()
                send(piece(d, x, device[2]), land.at[d, x, p], device, numbers[(x, rel)])
        return numbers

    def landed(land, part, numbers):
        for d, x, rel, device in routes:
            if d == part:
                arrived(land.at[d, x, device[2]], device, numbers[(x, rel)])

    x_spread = [spread(xr, d, lambda d, x, q: xs.at[d, q]) for d in range(2)]
    c_spread = [spread(cr, d, lambda d, x, q: cs.at[d, q]) for d in range(2)]
    xr[0, 0, p] = xs[0, p]
    cr[0, 0, p] = cs[0, p]

    def rows(ref, at, n):
        return ref.at[pl.ds(at, n)]

    pieces = [(x, q) for x in range(2) for q in range(2)]
    steps = [
        (which, k) for k in range(1, HOPS + 1) for which in range(2 if k < HOPS else 1)
    ]

    class Gather:
        def __init__(self, land, numbers, buf):
            self.land, self.numbers, self.buf = land, numbers, buf
            self.n = {(part, which, k): ticket() for which, k in steps for part in range(2)}
            self.s = [ticket() for _ in range(HOPS + 1)]

        def place(self, part, which, k):
            return rows(self.buf, group_at(k) + BLOCK * which * (k > 0) + PART * part, PART)

        def forward(self, part, which, k, to, device):
            send(self.place(part, which, k), self.place(part, which, to), device, self.n[(part, which, to)])

        def own(self, part):
            landed(self.land, part, self.numbers[part])
            for i, (x, q) in enumerate(pieces):
                wide[4 * i : 4 * i + 4, :] = self.land[part, x, q].astype(F32)
            self.buf[PART * part : PART * part + PART, :] = wide[...].astype(BF)

        def first(self, part):
            self.forward(part, 0, 0, 2, up2)
            self.forward(part, 1, 0, 2, down2)
            self.forward(part, 0, 0, 1, up)
            self.forward(part, 1, 0, 1, down)

        def here(self, part, k):
            for which, device in ((0, up), (1, down)):
                n = self.n.get((part, which, k))
                if n is not None:
                    arrived(self.place(part, which, k), device, n)

        def second(self, part):
            self.here(part, 2)
            self.forward(part, 0, 2, 4, up2)
            self.forward(part, 0, 2, 3, up)
            self.forward(part, 1, 2, 3, down)

        def hand(self, k):
            at, n = group_at(k), group_own(k)
            send(rows(self.buf, at, n), rows(self.buf, at + n, n), sib, self.s[k])

        def group(self, k):
            at, n = group_at(k), group_own(k)
            arrived(rows(self.buf, at + n, n), sib, self.s[k])

    class Inner:
        def __init__(self, gather, weight, own, out, inn):
            self.gather, self.weight = gather, weight
            self.own, self.out, self.inn = own, out, inn
            self.n = [ticket() for _ in range(HOPS + 1)]

        def make(self, k):
            self.gather.group(k)
            at, n = group_at(k), 2 * group_own(k)
            part = nt(self.gather.buf[at : at + n, :], self.weight[...])
            self.out[at : at + n, :] = part.astype(BF)
            send(rows(self.out, at, n), rows(self.inn, at, n), pair, self.n[k])
            self.own[at : at + n, :] = part

        def total(self, k):
            at, n = group_at(k), 2 * group_own(k)
            arrived(rows(self.inn, at, n), pair, self.n[k])
            return self.own[at : at + n, :] + self.inn[at : at + n, :].astype(F32)

    class Scatter:
        def __init__(self, left, weight, own, out, inn, go_on, come, base, stage, land, dest):
            self.left, self.weight = left, weight
            self.own, self.out, self.inn = own, out, inn
            self.go_on, self.come, self.base = go_on, come, base
            self.stage, self.land, self.dest = stage, land, dest
            self.s = [ticket() for _ in range(HOPS + 1)]
            self.n = {(part, which, k): ticket() for which, k in steps for part in range(2)}
            self.numbers = {}

        def make(self, k):
            at, n = group_at(k), group_own(k)
            term = nn(self.left[at : at + 2 * n, :], self.weight[...])
            to = own_at(k)
            self.out[to : to + n, :] = term[n:, :].astype(BF)
            send(rows(self.out, to, n), rows(self.inn, to, n), sib, self.s[k])
            self.own[to : to + n, :] = term[:n, :]

        def meet(self, k):
            arrived(rows(self.inn, own_at(k), group_own(k)), sib, self.s[k])

        def sums(self, part, which, k, joins):
            at = own_at(k) + BLOCK * which * (k > 0) + PART * part
            total = self.own[at : at + PART, :] + self.inn[at : at + PART, :].astype(F32)
            for side, j in joins:
                was = own_at(j) + BLOCK * side + PART * part
                arrived(rows(self.come, was, PART), sib, self.n[(part, side, j)])
                total += self.come[was : was + PART, :].astype(F32)
            return total

        def push(self, part, which, k, device, joins=()):
            at = own_at(k) + BLOCK * which + PART * part
            self.go_on[at : at + PART, :] = self.sums(part, which, k, joins).astype(BF)
            send(rows(self.go_on, at, PART), rows(self.come, at, PART), device, self.n[(part, which, k)])

        def first(self, part):
            self.push(part, 0, 4, down2)
            self.push(part, 0, 3, down)
            self.push(part, 1, 3, up)

        def near(self, part):
            self.push(part, 0, 1, down)
            self.push(part, 1, 1, up)

        def second(self, part):
            self.push(part, 1, 2, up2, ((1, 3),))
            self.push(part, 0, 2, down2, ((0, 3), (0, 4)))

        def last(self, part):
            wide[...] = self.sums(part, 0, 0, ((0, 1), (1, 1), (1, 2), (0, 2)))
            for i, (x, q) in enumerate(pieces):
                self.stage[part, x, q] = wide[4 * i : 4 * i + 4, :].astype(BF)
            self.numbers[part] = spread(self.land, part, lambda d, x, q: self.stage.at[d, x, q])
            if part == 0:
                self.land[0, 0, p] = self.stage[0, 0, p]

        def deliver(self, part):
            landed(self.land, part, self.numbers[part])
            for h in range(2):
                span = slice(h * half, (h + 1) * half)
                self.dest[part, :, span] = (
                    self.base[part, :, span].astype(F32)
                    + self.land[part, 0, h].astype(F32)
                    + self.land[part, 1, h].astype(F32)
                ).astype(BF)

    def bend(k):
        at, n = group_at(k), 2 * group_own(k)
        v = hid.total(k)
        square = v * v
        th = jnp.tanh(ROOT * (v + CUBE * (square * v)))
        gate = 0.5 * (1.0 + th)
        act[at : at + n, :] = (v * gate).astype(BF)
        slope[at : at + n, :] = gate + 0.5 * v * (1.0 - th * th) * (
            ROOT * (1.0 + 3.0 * CUBE * square)
        )

    def back(k):
        at, n = group_at(k), 2 * group_own(k)
        grd[at : at + n, :] = (err.total(k) * slope[at : at + n, :]).astype(BF)

    A, B = 0, 1
    gx, gc = Gather(xr, x_spread, X), Gather(cr, c_spread, C)
    hid = Inner(gx, w1, h_own, h_out, h_in)
    err = Inner(gc, w2, e_own, e_out, e_in)
    sc_p = Scatter(act, w2, po, ps, pr, sp, rp, x_in, ys, yr, res)
    sc_q = Scatter(grd, w1, qo, qs, qr, sq, rq, c_in, ds, dr, dx)

    gx.own(A)
    gx.first(A)
    gx.own(B)
    gx.first(B)
    gx.hand(0)
    gc.own(A)
    gc.own(B)
    load1.wait()
    load2.wait()
    gx.second(A)
    gc.first(A)
    gx.second(B)
    gc.first(B)
    gc.hand(0)
    hid.make(0)
    gx.here(A, 1)
    gx.here(B, 1)
    gx.hand(1)
    gx.hand(2)
    hid.make(1)
    hid.make(2)
    gc.second(A)
    for k in (3, 4):
        gx.here(A, k)
        gx.here(B, k)
        gx.hand(k)
    gc.second(B)
    hid.make(3)
    hid.make(4)
    gc.here(A, 1)
    gc.here(B, 1)
    gc.hand(1)
    gc.hand(2)
    err.make(0)
    bend(0)
    bend(1)
    bend(2)
    err.make(1)
    err.make(2)
    bend(3)
    bend(4)
    sc_p.make(4)
    sc_p.make(3)
    for k in (3, 4):
        gc.here(A, k)
        gc.here(B, k)
        gc.hand(k)
    sc_p.meet(4)
    sc_p.meet(3)
    sc_p.first(B)
    sc_p.first(A)
    err.make(3)
    err.make(4)
    sc_p.make(1)
    sc_p.make(2)
    sc_p.make(0)
    sc_p.meet(1)
    sc_p.near(B)
    sc_p.near(A)
    for k in range(5):
        back(k)
    sc_q.make(4)
    sc_q.make(3)
    sc_p.meet(2)
    sc_p.second(B)
    sc_p.second(A)
    sc_q.meet(4)
    sc_q.meet(3)
    sc_q.first(B)
    sc_q.first(A)
    sc_q.make(1)
    sc_q.make(2)
    sc_q.make(0)
    sc_q.meet(1)
    sc_q.near(B)
    sc_q.near(A)
    sc_q.meet(2)
    go[...] = tn(act[...], C[...]).astype(BF)
    store1 = pltpu.make_async_copy(go, go_hbm, local_sem.at[2])
    store1.start()
    sc_q.second(B)
    sc_q.second(A)
    sc_p.meet(0)
    sc_p.last(B)
    sc_p.last(A)
    gi[...] = tn(grd[...], X[...]).astype(BF)
    store2 = pltpu.make_async_copy(gi, gi_hbm, local_sem.at[3])
    store2.start()
    sc_q.meet(0)
    sc_q.last(B)
    sc_q.last(A)
    for part in (A, B):
        sc_p.deliver(part)
    for part in (A, B):
        sc_q.deliver(part)
    for copy in sent:
        copy.wait_send()
    store1.wait()
    store2.wait()


def write_out(*refs):
    n = len(refs) // 2
    copies = [
        pltpu.make_async_copy(src, dst, refs[-1].at[i]) for i, (src, dst) in enumerate(zip(refs[:n], refs[n : 2 * n]))
    ]
    for copy in copies:
        copy.start()
    for copy in copies:
        copy.wait()


def on_device(acts, cotangent, w_in, w_out):
    _, hidden, half = w_out.shape
    d_model = 2 * half
    every = EVERY
    v = pltpu.VMEM
    stage = v((2, 2, 4, half), BF)
    land = v((2, 2, 2, 4, half), BF)
    inner = [v((every, hidden), F32), v((every, hidden), BF), v((every, hidden), BF)]
    own = EVERY // 2
    outer = [v((own, half), F32)] + [v((own, half), BF)] * 4
    any_place = pl.BlockSpec(memory_space=pl.ANY)
    here = pl.BlockSpec(memory_space=pltpu.VMEM)
    made = pl.pallas_call(
        kernel,
        out_shape=(
            jax.ShapeDtypeStruct((2, 4, d_model), BF),
            jax.ShapeDtypeStruct((2, 4, d_model), BF),
            jax.ShapeDtypeStruct((hidden, half), BF),
            jax.ShapeDtypeStruct((hidden, half), BF),
        ),
        in_specs=[pl.BlockSpec(memory_space=pltpu.HBM)] * 4,
        out_specs=(here, here, any_place, any_place),
        scratch_shapes=[v((2, 4, d_model), BF)] * 2
        + [stage, land] * 2
        + [land] * 4
        + [v((16, half), F32)]
        + [v((every, half), BF)] * 2
        + [v((hidden, half), BF)] * 4
        + inner * 2
        + [v((every, hidden), F32), v((every, hidden), BF), v((every, hidden), BF)]
        + outer * 2
        + [
            pltpu.SemaphoreType.DMA((COPIES,)),
            pltpu.SemaphoreType.DMA((COPIES,)),
            pltpu.SemaphoreType.DMA((6,)),
        ],
        compiler_params=pltpu.CompilerParams(
            collective_id=0, has_side_effects=True, vmem_limit_bytes=63 * 1024 * 1024
        ),
        cost_estimate=pl.CostEstimate(
            flops=12 * every * hidden * half, bytes_accessed=8 * hidden * half, transcendentals=every * hidden
        ),
    )(acts[0], cotangent[0], jnp.swapaxes(w_in[0], 0, 1), w_out[0])
    result, d_acts, g_in, g_out = pl.pallas_call(
        write_out,
        out_shape=[jax.ShapeDtypeStruct(a.shape, a.dtype) for a in made],
        in_specs=[here] * 4,
        out_specs=[pl.BlockSpec(memory_space=pltpu.HBM)] * 4,
        scratch_shapes=[pltpu.SemaphoreType.DMA((4,))],
    )(*made)
    return (result[None], d_acts[None], jnp.swapaxes(g_in, 0, 1)[None], g_out[None])


def solution(mesh):
    placed = (
        P("section", None, ("tensor", "dp"), None),
        P("section", None, ("tensor", "dp"), None),
        P("section", "dp", "tensor"),
        P("section", "tensor", "dp"),
    )
    return jax.shard_map(on_device, mesh=mesh, in_specs=placed, out_specs=placed, check_vma=False)
```

```python
import jax
import jax.numpy as jnp
from jax import lax
from jax.experimental import pallas as pl
from jax.experimental.pallas import tpu as pltpu
from jax.sharding import PartitionSpec as P

MESH = pl.DeviceIdType.MESH
BF, F32 = jnp.bfloat16, jnp.float32
RING = 8
HOPS = RING // 2
BLOCK = 32
PART = BLOCK // 2
EVERY = 2 * RING * BLOCK
COPIES = 114
ROOT = 0.7978845608028654
CUBE = 0.044715


def group_own(k):
    return BLOCK if k in (0, HOPS) else 2 * BLOCK


def own_at(k):
    return sum(group_own(i) for i in range(k))


def group_at(k):
    return 2 * own_at(k)


def nt(a, b):
    return lax.dot_general(a, b, (((1,), (1,)), ((), ())), preferred_element_type=F32)


def nn(a, b):
    return lax.dot_general(a, b, (((1,), (0,)), ((), ())), preferred_element_type=F32)


def tn(a, b):
    return lax.dot_general(a, b, (((0,), (0,)), ((), ())), preferred_element_type=F32)


def kernel(
    x_hbm, c_hbm, w1_hbm, w2_hbm,
    res, dx, gi_hbm, go_hbm,
    x_in, c_in, xs, xr, cs, cr, ys, yr, ds, dr, wide, X, C, w1, w2, gi, go,
    h_own, h_out, h_in, e_own, e_out, e_in, slope, act, grd,
    po, ps, pr, sp, rp, qo, qs, qr, sq, rq,
    send_sem, recv_sem, local_sem,
):
    s, t, p = (lax.axis_index(a) for a in ("section", "tensor", "dp"))
    sections = lax.axis_size("section")
    core = t % 2
    z = (t // 2) % RING
    x_hi = t // (2 * RING)
    turn = 1 - 2 * core

    def at_z(step):
        return (s, x_hi * 2 * RING + ((z + RING + step) % RING) * 2 + core, p)

    up, down, up2, down2 = at_z(turn), at_z(-turn), at_z(2 * turn), at_z(-2 * turn)
    sib = (s, t + turn, p)
    other_t = (t + 2 * RING) % (4 * RING)
    mirror = sections - 1 - s
    routes = [
        (d, x, rel, ((s, mirror)[d], (t, other_t)[x], p + rel - 2 * rel * p))
        for d in range(2)
        for x in range(2)
        for rel in range(2)
        if d + x + rel > 0
    ]
    pair = routes[0][3]
    half = w1.shape[1]

    barrier = pltpu.get_barrier_semaphore()
    peers = [up, down, up2, down2, sib] + [route[3] for route in routes]
    for peer in peers:
        pl.semaphore_signal(barrier, inc=1, device_id=peer, device_id_type=MESH)

    load_x = pltpu.make_async_copy(x_hbm, x_in, local_sem.at[4])
    load_c = pltpu.make_async_copy(c_hbm, c_in, local_sem.at[5])
    load_x.start()
    load_c.start()
    load1 = pltpu.make_async_copy(w1_hbm, w1, local_sem.at[0])
    load2 = pltpu.make_async_copy(w2_hbm, w2, local_sem.at[1])
    load1.start()
    load2.start()

    sent = []
    count = [0]

    def ticket():
        count[0] += 1
        return count[0] - 1

    def send(src, dst, device, n):
        copy = pltpu.make_async_remote_copy(
            src_ref=src, dst_ref=dst, send_sem=send_sem.at[n], recv_sem=recv_sem.at[n],
            device_id=device, device_id_type=MESH,
        )
        copy.start()
        sent.append(copy)

    def arrived(dst, device, n):
        pltpu.make_async_remote_copy(
            src_ref=dst, dst_ref=dst, send_sem=send_sem.at[n], recv_sem=recv_sem.at[n],
            device_id=device, device_id_type=MESH,
        ).wait_recv()

    for load, source, stage in ((load_x, x_in, xs), (load_c, c_in, cs)):
        load.wait()
        for d in range(2):
            for h in range(2):
                stage[d, h] = source[d, :, h * half : (h + 1) * half]
    pl.semaphore_wait(barrier, len(peers))

    def spread(land, part, piece):
        numbers = {}
        for d, x, rel, device in routes:
            if d == part:
                numbers[(x, rel)] = ticket()
                send(piece(d, x, device[2]), land.at[d, x, p], device, numbers[(x, rel)])
        return numbers

    def landed(land, part, numbers):
        for d, x, rel, device in routes:
            if d == part:
                arrived(land.at[d, x, device[2]], device, numbers[(x, rel)])

    x_spread = {d: spread(xr, d, lambda d, x, q: xs.at[d, q]) for d in (1, 0)}
    c_spread = {d: spread(cr, d, lambda d, x, q: cs.at[d, q]) for d in (1, 0)}
    xr[0, 0, p] = xs[0, p]
    cr[0, 0, p] = cs[0, p]

    def rows(ref, at, n):
        return ref.at[pl.ds(at, n)]

    pieces = [(x, q) for x in range(2) for q in range(2)]
    steps = [
        (which, k) for k in range(1, HOPS + 1) for which in range(2 if k < HOPS else 1)
    ]

    class Gather:
        def __init__(self, land, numbers, buf):
            self.land, self.numbers, self.buf = land, numbers, buf
            self.n = {(part, which, k): ticket() for which, k in steps for part in range(2)}
            self.s = [ticket() for _ in range(HOPS + 1)]

        def place(self, part, which, k):
            return rows(self.buf, group_at(k) + BLOCK * which * (k > 0) + PART * part, PART)

        def forward(self, part, k):
            for which, device in ((0, up), (1, down)):
                n = self.n.get((part, which, k + 1))
                if n is not None:
                    send(self.place(part, which, k), self.place(part, which, k + 1), device, n)

        def own(self, part):
            landed(self.land, part, self.numbers[part])
            for i, (x, q) in enumerate(pieces):
                wide[4 * i : 4 * i + 4, :] = self.land[part, x, q].astype(F32)
            self.buf[PART * part : PART * part + PART, :] = wide[...].astype(BF)
            self.forward(part, 0)

        def step(self, part, k):
            for which, device in ((0, up), (1, down)):
                n = self.n.get((part, which, k))
                if n is not None:
                    arrived(self.place(part, which, k), device, n)
            self.forward(part, k)

        def hand(self, k):
            at, n = group_at(k), group_own(k)
            send(rows(self.buf, at, n), rows(self.buf, at + n, n), sib, self.s[k])

        def group(self, k):
            at, n = group_at(k), group_own(k)
            arrived(rows(self.buf, at + n, n), sib, self.s[k])

    class Inner:
        def __init__(self, gather, weight, own, out, inn):
            self.gather, self.weight = gather, weight
            self.own, self.out, self.inn = own, out, inn
            self.n = [ticket() for _ in range(HOPS + 1)]

        def make(self, k):
            self.gather.group(k)
            at, n = group_at(k), 2 * group_own(k)
            part = nt(self.gather.buf[at : at + n, :], self.weight[...])
            self.out[at : at + n, :] = part.astype(BF)
            send(rows(self.out, at, n), rows(self.inn, at, n), pair, self.n[k])
            self.own[at : at + n, :] = part

        def total(self, k):
            at, n = group_at(k), 2 * group_own(k)
            arrived(rows(self.inn, at, n), pair, self.n[k])
            return self.own[at : at + n, :] + self.inn[at : at + n, :].astype(F32)

    class Scatter:
        def __init__(self, left, weight, own, out, inn, go_on, come, base, stage, land, dest):
            self.left, self.weight = left, weight
            self.own, self.out, self.inn = own, out, inn
            self.go_on, self.come, self.base = go_on, come, base
            self.stage, self.land, self.dest = stage, land, dest
            self.s = [ticket() for _ in range(HOPS + 1)]
            self.n = {(part, which, k): ticket() for which, k in steps for part in range(2)}
            self.numbers = {}

        def make(self, k):
            at, n = group_at(k), group_own(k)
            term = nn(self.left[at : at + 2 * n, :], self.weight[...])
            to = own_at(k)
            self.out[to : to + n, :] = term[n:, :].astype(BF)
            send(rows(self.out, to, n), rows(self.inn, to, n), sib, self.s[k])
            self.own[to : to + n, :] = term[:n, :]

        def meet(self, k):
            arrived(rows(self.inn, own_at(k), group_own(k)), sib, self.s[k])

        def sums(self, part, which, k, joins):
            at = own_at(k) + BLOCK * which * (k > 0) + PART * part
            total = self.own[at : at + PART, :] + self.inn[at : at + PART, :].astype(F32)
            for side, j in joins:
                was = own_at(j) + BLOCK * side + PART * part
                arrived(rows(self.come, was, PART), sib, self.n[(part, side, j)])
                total += self.come[was : was + PART, :].astype(F32)
            return total

        def push(self, part, which, k, device, joins=()):
            at = own_at(k) + BLOCK * which + PART * part
            self.go_on[at : at + PART, :] = self.sums(part, which, k, joins).astype(BF)
            send(rows(self.go_on, at, PART), rows(self.come, at, PART), device, self.n[(part, which, k)])

        def far3(self, part):
            self.push(part, 0, 3, down)
            self.push(part, 1, 3, up)

        def far4(self, part):
            self.push(part, 0, 4, down2)

        def a2(self, part):
            self.push(part, 0, 2, down, ((0, 3), (0, 4)))

        def b2(self, part):
            self.push(part, 1, 2, up, ((1, 3),))

        def a1(self, part):
            self.push(part, 0, 1, down, ((0, 2),))

        def b1(self, part):
            self.push(part, 1, 1, up, ((1, 2),))

        def last(self, part):
            wide[...] = self.sums(part, 0, 0, ((0, 1), (1, 1)))
            for i, (x, q) in enumerate(pieces):
                self.stage[part, x, q] = wide[4 * i : 4 * i + 4, :].astype(BF)
            self.numbers[part] = spread(self.land, part, lambda d, x, q: self.stage.at[d, x, q])
            if part == 0:
                self.land[0, 0, p] = self.stage[0, 0, p]

        def deliver(self, part):
            landed(self.land, part, self.numbers[part])
            for h in range(2):
                span = slice(h * half, (h + 1) * half)
                self.dest[part, :, span] = (
                    self.base[part, :, span].astype(F32)
                    + self.land[part, 0, h].astype(F32)
                    + self.land[part, 1, h].astype(F32)
                ).astype(BF)

    def bend(k):
        at, n = group_at(k), 2 * group_own(k)
        v = hid.total(k)
        square = v * v
        th = jnp.tanh(ROOT * (v + CUBE * (square * v)))
        gate = 0.5 * (1.0 + th)
        act[at : at + n, :] = (v * gate).astype(BF)
        slope[at : at + n, :] = gate + 0.5 * v * (1.0 - th * th) * (
            ROOT * (1.0 + 3.0 * CUBE * square)
        )

    def back(k):
        at, n = group_at(k), 2 * group_own(k)
        grd[at : at + n, :] = (err.total(k) * slope[at : at + n, :]).astype(BF)

    A, B = 0, 1
    gx, gc = Gather(xr, x_spread, X), Gather(cr, c_spread, C)
    hid = Inner(gx, w1, h_own, h_out, h_in)
    err = Inner(gc, w2, e_own, e_out, e_in)
    sc_p = Scatter(act, w2, po, ps, pr, sp, rp, x_in, ys, yr, res)
    sc_q = Scatter(grd, w1, qo, qs, qr, sq, rq, c_in, ds, dr, dx)

    gx.own(A)
    gc.own(A)
    gx.own(B)
    gx.hand(0)
    load1.wait()
    load2.wait()
    gx.step(A, 1)
    gc.step(A, 1)
    gc.own(B)
    gc.hand(0)
    for k in range(1, HOPS):
        hid.make(k - 1)
        gx.step(B, k)
        gx.hand(k)
        gx.step(A, k + 1)
        gc.step(A, k + 1)
        gc.step(B, k)
        gc.hand(k)
        err.make(k - 1)
        if k > 1:
            bend(k - 2)
        if k > 2:
            back(k - 3)
    hid.make(3)
    gx.step(B, 4)
    gx.hand(4)
    err.make(3)
    bend(2)
    hid.make(4)
    gc.step(B, 4)
    gc.hand(4)
    bend(3)
    sc_p.make(3)
    err.make(4)
    back(3)
    sc_q.make(3)
    sc_p.meet(3)
    sc_p.far3(B)
    sc_p.far3(A)
    sc_q.meet(3)
    sc_q.far3(B)
    sc_q.far3(A)
    bend(4)
    sc_p.make(4)
    back(4)
    sc_q.make(4)
    sc_p.make(2)
    back(1)
    back(2)
    sc_p.meet(4)
    sc_p.far4(B)
    sc_p.far4(A)
    sc_q.meet(4)
    sc_q.far4(B)
    sc_q.far4(A)
    sc_q.make(2)
    sc_p.meet(2)
    sc_p.b2(B)
    sc_p.b2(A)
    sc_q.meet(2)
    sc_q.b2(B)
    sc_q.b2(A)
    for k in (1, 0):
        sc_p.make(k)
        sc_q.make(k)
    go[...] = tn(act[...], C[...]).astype(BF)
    store1 = pltpu.make_async_copy(go, go_hbm, local_sem.at[2])
    store1.start()
    for part in (B, A):
        sc_p.a2(part)
        sc_q.a2(part)
    sc_p.meet(1)
    sc_q.meet(1)
    for part in (B, A):
        sc_p.b1(part)
        sc_q.b1(part)
    gi[...] = tn(grd[...], X[...]).astype(BF)
    store2 = pltpu.make_async_copy(gi, gi_hbm, local_sem.at[3])
    store2.start()
    for part in (B, A):
        sc_p.a1(part)
        sc_q.a1(part)
    sc_p.meet(0)
    sc_q.meet(0)
    sc_p.last(B)
    sc_q.last(B)
    sc_p.last(A)
    sc_q.last(A)
    for part in (A, B):
        sc_p.deliver(part)
        sc_q.deliver(part)
    for copy in sent:
        copy.wait_send()
    store1.wait()
    store2.wait()


def write_out(a, b, c, d, a_out, b_out, c_out, d_out, a_mid, b_mid, c_mid, d_mid, sem):
    half = c.shape[1] // 2 // 128 * 128
    parts = [(c, c_mid, c_out), (d, d_mid, d_out)]
    moves = [
        (src.at[:, span], mid.at[:, span], dst.at[:, span])
        for src, mid, dst in parts
        for span in (pl.ds(0, half), pl.ds(half, c.shape[1] - half))
    ] + [(a, a_mid, a_out), (b, b_mid, b_out)]
    loads = [pltpu.make_async_copy(m[0], m[1], sem.at[0, n]) for n, m in enumerate(moves)]
    stores = [pltpu.make_async_copy(m[1], m[2], sem.at[1, n]) for n, m in enumerate(moves)]
    for load in loads:
        load.start()
    for load, store in zip(loads, stores):
        load.wait()
        store.start()
    for store in stores:
        store.wait()


def on_device(acts, cotangent, w_in, w_out):
    _, hidden, half = w_out.shape
    d_model = 2 * half
    every = EVERY
    v = pltpu.VMEM
    stage = v((2, 2, 4, half), BF)
    land = v((2, 2, 2, 4, half), BF)
    inner = [v((every, hidden), F32), v((every, hidden), BF), v((every, hidden), BF)]
    own = EVERY // 2
    outer = [v((own, half), F32)] + [v((own, half), BF)] * 4
    any_place = pl.BlockSpec(memory_space=pl.ANY)
    here = pl.BlockSpec(memory_space=pltpu.VMEM)
    made = pl.pallas_call(
        kernel,
        out_shape=(
            jax.ShapeDtypeStruct((2, 4, d_model), BF),
            jax.ShapeDtypeStruct((2, 4, d_model), BF),
            jax.ShapeDtypeStruct((hidden, half), BF),
            jax.ShapeDtypeStruct((hidden, half), BF),
        ),
        in_specs=[pl.BlockSpec(memory_space=pltpu.HBM)] * 4,
        out_specs=(here, here, any_place, any_place),
        scratch_shapes=[v((2, 4, d_model), BF)] * 2
        + [stage, land] * 2
        + [land] * 4
        + [v((16, half), F32)]
        + [v((every, half), BF)] * 2
        + [v((hidden, half), BF)] * 4
        + inner * 2
        + [v((every, hidden), F32), v((every, hidden), BF), v((every, hidden), BF)]
        + outer * 2
        + [
            pltpu.SemaphoreType.DMA((COPIES,)),
            pltpu.SemaphoreType.DMA((COPIES,)),
            pltpu.SemaphoreType.DMA((6,)),
        ],
        compiler_params=pltpu.CompilerParams(
            collective_id=0, has_side_effects=True, vmem_limit_bytes=63 * 1024 * 1024
        ),
        cost_estimate=pl.CostEstimate(
            flops=12 * every * hidden * half, bytes_accessed=8 * hidden * half, transcendentals=every * hidden
        ),
    )(acts[0], cotangent[0], jnp.swapaxes(w_in[0], 0, 1), w_out[0])
    result, d_acts, g_in, g_out = pl.pallas_call(
        write_out,
        out_shape=[jax.ShapeDtypeStruct(a.shape, a.dtype) for a in made],
        in_specs=[pl.BlockSpec(memory_space=pltpu.HBM)] * 4,
        out_specs=[pl.BlockSpec(memory_space=pltpu.HBM)] * 4,
        scratch_shapes=[v(a.shape, a.dtype) for a in made] + [pltpu.SemaphoreType.DMA((2, 6))],
    )(*made)
    return (result[None], d_acts[None], jnp.swapaxes(g_in, 0, 1)[None], g_out[None])


def solution(mesh):
    placed = (
        P("section", None, ("tensor", "dp"), None),
        P("section", None, ("tensor", "dp"), None),
        P("section", "dp", "tensor"),
        P("section", "tensor", "dp"),
    )
    return jax.shard_map(on_device, mesh=mesh, in_specs=placed, out_specs=placed, check_vma=False)
```

```python
import jax
import jax.numpy as jnp
from jax import lax
from jax.experimental import pallas as pl
from jax.experimental.pallas import tpu as pltpu
from jax.sharding import PartitionSpec as P

MESH = pl.DeviceIdType.MESH
BF, F32 = jnp.bfloat16, jnp.float32
RING = 8
HOPS = RING // 2
BLOCK = 32
PART = BLOCK // 2
EVERY = 2 * RING * BLOCK
COPIES = 114
ROOT = 0.7978845608028654
CUBE = 0.044715


def group_own(k):
    return BLOCK if k in (0, HOPS) else 2 * BLOCK


def own_at(k):
    return sum(group_own(i) for i in range(k))


def group_at(k):
    return 2 * own_at(k)


def nt(a, b):
    return lax.dot_general(a, b, (((1,), (1,)), ((), ())), preferred_element_type=F32)


def nn(a, b):
    return lax.dot_general(a, b, (((1,), (0,)), ((), ())), preferred_element_type=F32)


def tn(a, b):
    return lax.dot_general(a, b, (((0,), (0,)), ((), ())), preferred_element_type=F32)


def kernel(
    x_hbm, c_hbm, w1_hbm, w2_hbm,
    res, dx, gi_hbm, go_hbm,
    x_in, c_in, xs, xr, cs, cr, ys, yr, ds, dr, wide, X, C, w1, w2, gi, go,
    h_own, h_out, h_in, e_own, e_out, e_in, slope, act, grd,
    po, ps, pr, sp, rp, qo, qs, qr, sq, rq,
    send_sem, recv_sem, local_sem,
):
    s, t, p = (lax.axis_index(a) for a in ("section", "tensor", "dp"))
    sections = lax.axis_size("section")
    core = t % 2
    z = (t // 2) % RING
    x_hi = t // (2 * RING)
    turn = 1 - 2 * core

    def at_z(step):
        return (s, x_hi * 2 * RING + ((z + RING + step) % RING) * 2 + core, p)

    up, down, up2, down2 = at_z(turn), at_z(-turn), at_z(2 * turn), at_z(-2 * turn)
    sib = (s, t + turn, p)
    other_t = (t + 2 * RING) % (4 * RING)
    mirror = sections - 1 - s
    routes = [
        (d, x, rel, ((s, mirror)[d], (t, other_t)[x], p + rel - 2 * rel * p))
        for d in range(2)
        for x in range(2)
        for rel in range(2)
        if d + x + rel > 0
    ]
    pair = routes[0][3]
    half = w1.shape[1]

    barrier = pltpu.get_barrier_semaphore()
    peers = [up, down, up2, down2, sib] + [route[3] for route in routes]
    for peer in peers:
        pl.semaphore_signal(barrier, inc=1, device_id=peer, device_id_type=MESH)

    load_x = pltpu.make_async_copy(x_hbm, x_in, local_sem.at[4])
    load_c = pltpu.make_async_copy(c_hbm, c_in, local_sem.at[5])
    load_x.start()
    load_c.start()
    load1 = pltpu.make_async_copy(w1_hbm, w1, local_sem.at[0])
    load2 = pltpu.make_async_copy(w2_hbm, w2, local_sem.at[1])
    load1.start()
    load2.start()

    sent = []
    count = [0]

    def ticket():
        count[0] += 1
        return count[0] - 1

    def send(src, dst, device, n):
        copy = pltpu.make_async_remote_copy(
            src_ref=src, dst_ref=dst, send_sem=send_sem.at[n], recv_sem=recv_sem.at[n],
            device_id=device, device_id_type=MESH,
        )
        copy.start()
        sent.append(copy)

    def arrived(dst, device, n):
        pltpu.make_async_remote_copy(
            src_ref=dst, dst_ref=dst, send_sem=send_sem.at[n], recv_sem=recv_sem.at[n],
            device_id=device, device_id_type=MESH,
        ).wait_recv()

    for load, source, stage in ((load_x, x_in, xs), (load_c, c_in, cs)):
        load.wait()
        for d in range(2):
            for h in range(2):
                stage[d, h] = source[d, :, h * half : (h + 1) * half]
    pl.semaphore_wait(barrier, len(peers))

    def spread(land, part, piece):
        numbers = {}
        for d, x, rel, device in routes:
            if d == part:
                numbers[(x, rel)] = ticket()
                send(piece(d, x, device[2]), land.at[d, x, p], device, numbers[(x, rel)])
        return numbers

    def landed(land, part, numbers):
        for d, x, rel, device in routes:
            if d == part:
                arrived(land.at[d, x, device[2]], device, numbers[(x, rel)])

    x_spread = {d: spread(xr, d, lambda d, x, q: xs.at[d, q]) for d in (1, 0)}
    c_spread = {d: spread(cr, d, lambda d, x, q: cs.at[d, q]) for d in (1, 0)}
    xr[0, 0, p] = xs[0, p]
    cr[0, 0, p] = cs[0, p]

    def rows(ref, at, n):
        return ref.at[pl.ds(at, n)]

    pieces = [(x, q) for x in range(2) for q in range(2)]
    steps = [
        (which, k) for k in range(1, HOPS + 1) for which in range(2 if k < HOPS else 1)
    ]

    class Gather:
        def __init__(self, land, numbers, buf):
            self.land, self.numbers, self.buf = land, numbers, buf
            self.n = {(part, which, k): ticket() for which, k in steps for part in range(2)}
            self.s = [ticket() for _ in range(HOPS + 1)]

        def place(self, part, which, k):
            return rows(self.buf, group_at(k) + BLOCK * which * (k > 0) + PART * part, PART)

        def forward(self, part, k):
            for which, device in ((0, up), (1, down)):
                n = self.n.get((part, which, k + 1))
                if n is not None:
                    send(self.place(part, which, k), self.place(part, which, k + 1), device, n)

        def own(self, part):
            landed(self.land, part, self.numbers[part])
            for i, (x, q) in enumerate(pieces):
                wide[4 * i : 4 * i + 4, :] = self.land[part, x, q].astype(F32)
            self.buf[PART * part : PART * part + PART, :] = wide[...].astype(BF)
            self.forward(part, 0)

        def step(self, part, k):
            for which, device in ((0, up), (1, down)):
                n = self.n.get((part, which, k))
                if n is not None:
                    arrived(self.place(part, which, k), device, n)
            self.forward(part, k)

        def hand(self, k):
            at, n = group_at(k), group_own(k)
            send(rows(self.buf, at, n), rows(self.buf, at + n, n), sib, self.s[k])

        def group(self, k):
            at, n = group_at(k), group_own(k)
            arrived(rows(self.buf, at + n, n), sib, self.s[k])

    class Inner:
        def __init__(self, gather, weight, own, out, inn):
            self.gather, self.weight = gather, weight
            self.own, self.out, self.inn = own, out, inn
            self.n = [ticket() for _ in range(HOPS + 1)]

        def make(self, k):
            self.gather.group(k)
            at, n = group_at(k), 2 * group_own(k)
            part = nt(self.gather.buf[at : at + n, :], self.weight[...])
            self.out[at : at + n, :] = part.astype(BF)
            send(rows(self.out, at, n), rows(self.inn, at, n), pair, self.n[k])
            self.own[at : at + n, :] = part

        def total(self, k):
            at, n = group_at(k), 2 * group_own(k)
            arrived(rows(self.inn, at, n), pair, self.n[k])
            return self.own[at : at + n, :] + self.inn[at : at + n, :].astype(F32)

    class Scatter:
        def __init__(self, left, weight, own, out, inn, go_on, come, base, stage, land, dest):
            self.left, self.weight = left, weight
            self.own, self.out, self.inn = own, out, inn
            self.go_on, self.come, self.base = go_on, come, base
            self.stage, self.land, self.dest = stage, land, dest
            self.s = [ticket() for _ in range(HOPS + 1)]
            self.n = {(part, which, k): ticket() for which, k in steps for part in range(2)}
            self.numbers = {}

        def make(self, k):
            at, n = group_at(k), group_own(k)
            term = nn(self.left[at : at + 2 * n, :], self.weight[...])
            to = own_at(k)
            self.out[to : to + n, :] = term[n:, :].astype(BF)
            send(rows(self.out, to, n), rows(self.inn, to, n), sib, self.s[k])
            self.own[to : to + n, :] = term[:n, :]

        def meet(self, k):
            arrived(rows(self.inn, own_at(k), group_own(k)), sib, self.s[k])

        def sums(self, part, which, k, joins):
            at = own_at(k) + BLOCK * which * (k > 0) + PART * part
            total = self.own[at : at + PART, :] + self.inn[at : at + PART, :].astype(F32)
            for side, j in joins:
                was = own_at(j) + BLOCK * side + PART * part
                arrived(rows(self.come, was, PART), sib, self.n[(part, side, j)])
                total += self.come[was : was + PART, :].astype(F32)
            return total

        def push(self, part, which, k, device, joins=()):
            at = own_at(k) + BLOCK * which + PART * part
            self.go_on[at : at + PART, :] = self.sums(part, which, k, joins).astype(BF)
            send(rows(self.go_on, at, PART), rows(self.come, at, PART), device, self.n[(part, which, k)])

        def far3(self, part):
            self.push(part, 0, 3, down)
            self.push(part, 1, 3, up)

        def far4(self, part):
            self.push(part, 0, 4, down2)

        def a2(self, part):
            self.push(part, 0, 2, down, ((0, 3), (0, 4)))

        def b2(self, part):
            self.push(part, 1, 2, up, ((1, 3),))

        def a1(self, part):
            self.push(part, 0, 1, down, ((0, 2),))

        def b1(self, part):
            self.push(part, 1, 1, up, ((1, 2),))

        def last(self, part):
            wide[...] = self.sums(part, 0, 0, ((0, 1), (1, 1)))
            for i, (x, q) in enumerate(pieces):
                self.stage[part, x, q] = wide[4 * i : 4 * i + 4, :].astype(BF)
            self.numbers[part] = spread(self.land, part, lambda d, x, q: self.stage.at[d, x, q])
            if part == 0:
                self.land[0, 0, p] = self.stage[0, 0, p]

        def deliver(self, part):
            landed(self.land, part, self.numbers[part])
            for h in range(2):
                span = slice(h * half, (h + 1) * half)
                self.dest[part, :, span] = (
                    self.base[part, :, span].astype(F32)
                    + self.land[part, 0, h].astype(F32)
                    + self.land[part, 1, h].astype(F32)
                ).astype(BF)

    def bend(k):
        at, n = group_at(k), 2 * group_own(k)
        v = hid.total(k)
        square = v * v
        th = jnp.tanh(ROOT * (v + CUBE * (square * v)))
        gate = 0.5 * (1.0 + th)
        act[at : at + n, :] = (v * gate).astype(BF)
        slope[at : at + n, :] = gate + 0.5 * v * (1.0 - th * th) * (
            ROOT * (1.0 + 3.0 * CUBE * square)
        )

    def back(k):
        at, n = group_at(k), 2 * group_own(k)
        grd[at : at + n, :] = (err.total(k) * slope[at : at + n, :]).astype(BF)

    A, B = 0, 1
    gx, gc = Gather(xr, x_spread, X), Gather(cr, c_spread, C)
    hid = Inner(gx, w1, h_own, h_out, h_in)
    err = Inner(gc, w2, e_own, e_out, e_in)
    sc_p = Scatter(act, w2, po, ps, pr, sp, rp, x_in, ys, yr, res)
    sc_q = Scatter(grd, w1, qo, qs, qr, sq, rq, c_in, ds, dr, dx)

    gx.own(A)
    gc.own(A)
    gx.own(B)
    gx.hand(0)
    load1.wait()
    load2.wait()
    gx.step(A, 1)
    gc.step(A, 1)
    gc.own(B)
    gc.hand(0)
    for k in range(1, HOPS):
        hid.make(k - 1)
        gx.step(B, k)
        gx.hand(k)
        gx.step(A, k + 1)
        gc.step(A, k + 1)
        gc.step(B, k)
        gc.hand(k)
        err.make(k - 1)
        if k > 1:
            bend(k - 2)
        if k > 2:
            back(k - 3)
    hid.make(3)
    gx.step(B, 4)
    gx.hand(4)
    err.make(3)
    bend(2)
    hid.make(4)
    gc.step(B, 4)
    gc.hand(4)
    bend(3)
    sc_p.make(3)
    err.make(4)
    back(3)
    sc_q.make(3)
    sc_p.meet(3)
    sc_p.far3(B)
    sc_p.far3(A)
    sc_q.meet(3)
    sc_q.far3(B)
    sc_q.far3(A)
    bend(4)
    sc_p.make(4)
    back(4)
    sc_q.make(4)
    sc_p.make(2)
    back(1)
    back(2)
    sc_p.meet(4)
    sc_p.far4(B)
    sc_p.far4(A)
    sc_q.meet(4)
    sc_q.far4(B)
    sc_q.far4(A)
    sc_q.make(2)
    sc_p.meet(2)
    sc_p.b2(B)
    sc_p.b2(A)
    sc_q.meet(2)
    sc_q.b2(B)
    sc_q.b2(A)
    for k in (1, 0):
        sc_p.make(k)
        sc_q.make(k)
    go[...] = tn(act[...], C[...]).astype(BF)
    store1 = pltpu.make_async_copy(go, go_hbm, local_sem.at[2])
    store1.start()
    for part in (B, A):
        sc_p.a2(part)
        sc_q.a2(part)
    sc_p.meet(1)
    sc_q.meet(1)
    for part in (B, A):
        sc_p.b1(part)
        sc_q.b1(part)
    gi[...] = tn(grd[...], X[...]).astype(BF)
    store2 = pltpu.make_async_copy(gi, gi_hbm, local_sem.at[3])
    store2.start()
    for part in (B, A):
        sc_p.a1(part)
        sc_q.a1(part)
    sc_p.meet(0)
    sc_q.meet(0)
    sc_p.last(B)
    sc_q.last(B)
    sc_p.last(A)
    sc_q.last(A)
    for part in (A, B):
        sc_p.deliver(part)
        sc_q.deliver(part)
    for copy in sent:
        copy.wait_send()
    store1.wait()
    store2.wait()


def write_out(a, b, c, d, a_out, b_out, c_out, d_out, a_mid, b_mid, c_mid, d_mid, sem):
    moves = [(c, c_mid, c_out), (d, d_mid, d_out), (a, a_mid, a_out), (b, b_mid, b_out)]
    loads = [pltpu.make_async_copy(m[0], m[1], sem.at[0, n]) for n, m in enumerate(moves)]
    stores = [pltpu.make_async_copy(m[1], m[2], sem.at[1, n]) for n, m in enumerate(moves)]
    for load in loads:
        load.start()
    for load, store in zip(loads, stores):
        load.wait()
        store.start()
    for store in stores:
        store.wait()


def on_device(acts, cotangent, w_in, w_out):
    _, hidden, half = w_out.shape
    d_model = 2 * half
    every = EVERY
    v = pltpu.VMEM
    stage = v((2, 2, 4, half), BF)
    land = v((2, 2, 2, 4, half), BF)
    inner = [v((every, hidden), F32), v((every, hidden), BF), v((every, hidden), BF)]
    own = EVERY // 2
    outer = [v((own, half), F32)] + [v((own, half), BF)] * 4
    any_place = pl.BlockSpec(memory_space=pl.ANY)
    here = pl.BlockSpec(memory_space=pltpu.VMEM)
    made = pl.pallas_call(
        kernel,
        out_shape=(
            jax.ShapeDtypeStruct((2, 4, d_model), BF),
            jax.ShapeDtypeStruct((2, 4, d_model), BF),
            jax.ShapeDtypeStruct((hidden, half), BF),
            jax.ShapeDtypeStruct((hidden, half), BF),
        ),
        in_specs=[pl.BlockSpec(memory_space=pltpu.HBM)] * 4,
        out_specs=(here, here, any_place, any_place),
        scratch_shapes=[v((2, 4, d_model), BF)] * 2
        + [stage, land] * 2
        + [land] * 4
        + [v((16, half), F32)]
        + [v((every, half), BF)] * 2
        + [v((hidden, half), BF)] * 4
        + inner * 2
        + [v((every, hidden), F32), v((every, hidden), BF), v((every, hidden), BF)]
        + outer * 2
        + [
            pltpu.SemaphoreType.DMA((COPIES,)),
            pltpu.SemaphoreType.DMA((COPIES,)),
            pltpu.SemaphoreType.DMA((6,)),
        ],
        compiler_params=pltpu.CompilerParams(
            collective_id=0, has_side_effects=True, vmem_limit_bytes=63 * 1024 * 1024
        ),
        cost_estimate=pl.CostEstimate(
            flops=12 * every * hidden * half, bytes_accessed=8 * hidden * half, transcendentals=every * hidden
        ),
    )(acts[0], cotangent[0], jnp.swapaxes(w_in[0], 0, 1), w_out[0])
    result, d_acts, g_in, g_out = pl.pallas_call(
        write_out,
        out_shape=[jax.ShapeDtypeStruct(a.shape, a.dtype) for a in made],
        in_specs=[pl.BlockSpec(memory_space=pltpu.HBM)] * 4,
        out_specs=[pl.BlockSpec(memory_space=pltpu.HBM)] * 4,
        scratch_shapes=[v(a.shape, a.dtype) for a in made] + [pltpu.SemaphoreType.DMA((2, 4))],
    )(*made)
    return (result[None], d_acts[None], jnp.swapaxes(g_in, 0, 1)[None], g_out[None])


def solution(mesh):
    placed = (
        P("section", None, ("tensor", "dp"), None),
        P("section", None, ("tensor", "dp"), None),
        P("section", "dp", "tensor"),
        P("section", "tensor", "dp"),
    )
    return jax.shard_map(on_device, mesh=mesh, in_specs=placed, out_specs=placed, check_vma=False)
```
